1024 devices in a mesh: shard: 64 (over z, x), rep: 16 (over y, core).
Axes of the slice: x: 8, y: 8, z: 8, core: 2. Of those that a mesh axis runs over, the one named last changes fastest.
Arguments:
- emb_table: float32 [128, 2048, 256], P('shard'), may hold values from -0.4 to 0.4
- accumulated: float32 [128, 2048], P('shard'), may hold values from 500 to 20000
- touched: int32 [128, 512], P('shard'), may hold values from 0 to 2047, as said below
- bag_slots: int32 [128, 16, 2048, 16], P('shard', 'rep'), may hold values from 0 to 511
- lengths: int32 [128, 16, 2048], P('shard', 'rep'), may hold values from 1 to 16
- cotangent: bfloat16 [16, 2048, 128, 128], P('rep', 'shard'), may hold values from -6 to 6
Outputs:
- interaction: bfloat16 [16, 2048, 128, 128], P('rep', 'shard')
- new_rows: float32 [128, 512, 256], P('shard')
The draws below stay inside these ranges and needn't reach their ends.
Inputs may be any that keep to these rules, and one draw needn't show every extreme that they name: `touched`: the 512 row ids of one table are distinct.
All inputs are finite; a program needn't handle non-finite values.
Results may differ from the reference program's by a relative error of at most 0.022.
Values may be sent and summed in bfloat16 or wider, within the bound.
A program may use at most 64 MiB of HBM per device.

```python
import math
import jax
import jax.numpy as jnp
from jax import lax

D = 256
ROWS = 2048
K = 512
L = 16
TABLES = 128
B_GRP = 2048
N_REP = 16


def draw_touched(key, part):
    key = jax.random.fold_in(key, 7)
    table_keys = jax.random.split(key, TABLES)

    def pick_rows(table_key):
        return jax.random.permutation(table_key, ROWS)[:K]
    return jax.vmap(pick_rows)(table_keys).astype(jnp.int32)


def place_ends(array, stream_key, least, top_value):
    place = [jax.random.randint(jax.random.fold_in(stream_key, axis), (), 0, length) for axis, length in enumerate(array.shape)]
    main_axis = array.shape.index(max(array.shape))
    neighbour = place[:main_axis] + [(place[main_axis] + 1) % array.shape[main_axis]] + place[main_axis + 1:]
    return array.at[tuple(place)].set(least).at[tuple(neighbour)].set(top_value)


def block_scale(key, dims, cuts, low, largest):
    factor_of = 1.0
    for position, blocks in cuts:
        heights = jax.random.uniform(jax.random.fold_in(jax.random.fold_in(key, 6), position), (blocks,), jnp.float32, low / len(cuts), largest / len(cuts))
        factor_of = factor_of * jnp.repeat(jnp.exp(heights), dims[position] // blocks).reshape((-1,) + (1,) * (len(dims) - 1 - position))
    return factor_of


def gaussian(rng, shape, deviation, most, shards=(), kind=jnp.bfloat16):
    level = block_scale(rng, shape, shards, -0.22, 0.18) if shards else 1.0
    drawn = jax.random.normal(rng, shape, jnp.float32) * deviation * level
    return jnp.minimum(jnp.maximum(drawn, -most), most).astype(kind)


def setup_inputs(seed: int = 0) -> dict:
    seeds = jax.random.split(jax.random.key(seed), 7)
    emb_table = gaussian(seeds[0], (TABLES, ROWS, D), 0.0625, 0.4, ((0, 64),), jnp.float32)
    accumulated = jnp.clip(jnp.exp(math.log(20000.0) - 3.6888795 * jax.random.uniform(seeds[1], (TABLES, ROWS), jnp.float32) ** block_scale(seeds[1], (TABLES, ROWS), ((0, 64),), -0.2, 0.2)), 500.0, 20000.0)
    touched = draw_touched(jax.random.fold_in(seeds[6], 71), 0)
    bag_slots = place_ends(jax.random.randint(seeds[3], (TABLES, N_REP, B_GRP, L), 0, K), jax.random.fold_in(seeds[3], 1), 0, K - 1).astype(jnp.int32)
    lengths = place_ends(jax.random.randint(seeds[4], (TABLES, N_REP, B_GRP), 1, L + 1), jax.random.fold_in(seeds[4], 1), 1, L).astype(jnp.int32)
    cotangent = gaussian(seeds[5], (N_REP, B_GRP, TABLES, TABLES), 1.0, 6.0, ((0, 16), (1, 64)))
    return dict(emb_table=emb_table, accumulated=accumulated, touched=touched, bag_slots=bag_slots, lengths=lengths, cotangent=cotangent)


learn_rate = 0.5
epsilon = 1e-08

def counts_block(slot_rows, length_rows, width):
    valid = jnp.arange(slot_rows.shape[-1], dtype=jnp.int32) < length_rows[..., None]
    hits = (slot_rows[..., None] == jnp.arange(width, dtype=jnp.int32)) & valid[..., None]
    return lax.optimization_barrier(jnp.sum(hits.astype(jnp.int32), axis=-2)).astype(jnp.bfloat16)

def table_counts(pair):
    return counts_block(pair[0], pair[1], K)

def reference(emb_table, accumulated, touched, bag_slots, lengths, cotangent):
    rows = jnp.take_along_axis(emb_table, touched[:, :, None], axis=1)
    rows_low = rows.astype(jnp.bfloat16)
    rows_wide = rows_low.astype(jnp.float32)

    def group(summed, inputs):
        slot_grp, len_grp, cot_grp = inputs
        counts = lax.map(table_counts, (slot_grp, len_grp))
        counts_wide = counts.astype(jnp.float32)
        pooled = jnp.einsum('tbk,tkd->tbd', counts_wide, rows_wide).astype(jnp.bfloat16)
        pooled_wide = pooled.astype(jnp.float32)
        products = jnp.einsum('tbd,sbd->bts', pooled_wide, pooled_wide).astype(jnp.bfloat16)
        cot_wide = cot_grp.astype(jnp.float32)
        dpool = (jnp.einsum('bts,sbd->tbd', cot_wide, pooled_wide) + jnp.einsum('bst,sbd->tbd', cot_wide, pooled_wide)).astype(jnp.bfloat16)
        grads = jnp.einsum('tbk,tbd->tkd', counts_wide, dpool.astype(jnp.float32))
        return (summed + grads, products)
    slot_groups = jnp.moveaxis(bag_slots, 1, 0)
    len_groups = jnp.moveaxis(lengths, 1, 0)
    start_sum = jnp.zeros((TABLES, K, D), jnp.float32)
    summed, interaction = lax.scan(group, start_sum, (slot_groups, len_groups, cotangent))
    acc_rows = jnp.take_along_axis(accumulated, touched, axis=1)
    acc_new = acc_rows + lax.optimization_barrier(jnp.mean(summed * summed, axis=-1))
    new_rows = rows - learn_rate * summed / (jnp.sqrt(acc_new)[..., None] + epsilon)
    return (interaction, new_rows)
```

```python
import functools

import jax
import jax.numpy as jnp
from jax import lax
from jax.experimental import pallas as pl
from jax.experimental.pallas import tpu as pltpu
from jax.sharding import PartitionSpec as P

MESH = pl.DeviceIdType.MESH
VMEM = pl.BlockSpec(memory_space=pltpu.VMEM)
learn_rate = 0.5
epsilon = 1e-08
LANES = 128
SUB = 16
CORES = 2


def gather_kernel(touched, acc, table, rows, acc_rows):
    t = pl.program_id(0)

    def eight(i, carry):
        for u in range(8):
            k = i * 8 + u
            idx = touched[t, k]
            rows[0, pl.ds(k, 1), :] = table[0, pl.ds(idx, 1), :]
            acc_rows[0, pl.ds(k, 1), :] = jnp.full((1, LANES), acc[t, idx], jnp.float32)
        return carry

    lax.fori_loop(0, touched.shape[1] // 8, eight, 0)


def gather_rows(emb_table, accumulated, touched):
    tabs, size, dim = emb_table.shape
    width = touched.shape[1]
    return pl.pallas_call(
        gather_kernel,
        grid=(tabs,),
        out_shape=(
            jax.ShapeDtypeStruct((tabs, width, dim), jnp.float32),
            jax.ShapeDtypeStruct((tabs, width, LANES), jnp.float32),
        ),
        in_specs=[
            pl.BlockSpec(memory_space=pltpu.SMEM),
            pl.BlockSpec(memory_space=pltpu.SMEM),
            pl.BlockSpec((1, size, dim), lambda t: (t, 0, 0)),
        ],
        out_specs=(
            pl.BlockSpec((1, width, dim), lambda t: (t, 0, 0)),
            pl.BlockSpec((1, width, LANES), lambda t: (t, 0, 0)),
        ),
        compiler_params=pltpu.CompilerParams(vmem_limit_bytes=32 << 20),
    )(touched, accumulated, emb_table)


def main_kernel(
    n_shard, n_rep, n_chunk,
    rows_ref, acc_ref, slot_ref, len_ref, cot_ref,
    inter_ref, new_ref,
    low, counts, pooled, got, mine, dmine, dsend, dgot,
    partial, part_low, half_got, half_low, y_got, sums, other,
    f_send, f_recv, f_own, b_send, b_recv, b_own,
    c_send, c_recv, y_send, y_recv, g_send, g_recv, h_send, h_recv,
):
    me = lax.axis_index("shard")
    rep = lax.axis_index("rep")
    core = lax.rem(rep, CORES)
    y = rep // CORES
    n_y = n_rep // CORES
    tabs, width, dim = rows_ref.shape
    batch = slot_ref.shape[2]
    own = batch // n_shard
    part = own // n_chunk
    n_tab = tabs * n_shard
    blocks = batch // LANES
    per_block = LANES // own
    groups = n_tab // SUB
    per_group = SUB // tabs
    sibling = rep + 1 - 2 * core

    barrier = pltpu.get_barrier_semaphore()

    def greet(i, carry):
        pl.semaphore_signal(
            barrier, inc=1, device_id={"shard": lax.rem(me + i, n_shard)}, device_id_type=MESH
        )
        return carry

    lax.fori_loop(1, n_shard, greet, 0)

    def greet_y(i, carry):
        peer = lax.rem(y + i, n_y) * CORES + core
        pl.semaphore_signal(barrier, inc=1, device_id={"rep": peer}, device_id_type=MESH)
        return carry

    lax.fori_loop(1, n_y, greet_y, 0)
    pl.semaphore_signal(barrier, inc=1, device_id={"rep": sibling}, device_id_type=MESH)

    low[...] = rows_ref[...].astype(jnp.bfloat16)
    pl.semaphore_wait(barrier, n_shard - 1 + n_y - 1 + 1)

    key0 = lax.broadcasted_iota(jnp.int32, (SUB, LANES), 0)
    one = jnp.ones((SUB, LANES), jnp.bfloat16)
    zero = jnp.zeros((SUB, LANES), jnp.bfloat16)

    def start_forward(c, dest):
        src = pooled.at[:, pl.ds(dest * own + c * part, part), :]

        @pl.when(dest == me)
        def _():
            pltpu.make_async_copy(
                src, got.at[pl.ds(me * tabs, tabs), pl.ds(c * part, part), :], f_own.at[c]
            ).start()

        @pl.when(dest != me)
        def _():
            pltpu.make_async_remote_copy(
                src_ref=src,
                dst_ref=got.at[pl.ds(me * tabs, tabs), pl.ds(c * part, part), :],
                send_sem=f_send.at[c],
                recv_sem=f_recv.at[c],
                device_id={"shard": dest},
                device_id_type=MESH,
            ).start()

    def block_of(i):
        away = lax.rem(i, 2) * ((i + 1) // 2) + (1 - lax.rem(i, 2)) * (blocks - i // 2)
        return lax.rem(me // per_block + away, blocks)

    def forward(i, carry):
        block = block_of(i)
        first = pl.multiple_of(block * LANES, LANES)
        for t in range(tabs):
            slots = slot_ref[t, :, pl.ds(first, LANES)]
            sizes = len_ref[t, :, pl.ds(first, LANES)]
            place = lax.broadcasted_iota(jnp.int32, slots.shape, 0)
            slots = jnp.where(place < sizes, slots, -1)
            wide = [
                jnp.broadcast_to(slots[l : l + 1], (SUB, LANES)).astype(jnp.int16)
                for l in range(slots.shape[0])
            ]
            for tile in range(width // SUB):
                key = (key0 + tile * SUB).astype(jnp.int16)
                terms = [jnp.where(key == w, one, zero) for w in wide]
                while len(terms) > 1:
                    terms = [a + b for a, b in zip(terms[::2], terms[1::2])]
                counts[t, pl.ds(tile * SUB, SUB), pl.ds(first, LANES)] = terms[0]
            block_counts = counts[t, :, pl.ds(first, LANES)]
            pooled[t, pl.ds(first, LANES), :] = lax.dot_general(
                block_counts, low[t], (((0,), (0,)), ((), ())), preferred_element_type=jnp.float32
            ).astype(jnp.bfloat16)
        for q in range(per_block):
            start_forward(0, block * per_block + q)
        return carry

    lax.fori_loop(0, blocks, forward, 0)

    for c in range(1, n_chunk):

        def rest(i, carry, c=c):
            block = block_of(i)
            for q in range(per_block):
                start_forward(c, block * per_block + q)
            return carry

        lax.fori_loop(0, blocks, rest, 0)

    swap_row = lax.broadcasted_iota(jnp.int32, (SUB * SUB, SUB * SUB), 0)
    swap_col = lax.broadcasted_iota(jnp.int32, (SUB * SUB, SUB * SUB), 1)
    swapped = lax.rem(swap_col, SUB) * SUB + swap_col // SUB
    swap = jnp.where(swap_row == swapped, 1.0, 0.0).astype(jnp.bfloat16)

    def swap_tile(tile):
        flat = tile.reshape(SUB * SUB, dim)
        out = jnp.dot(swap, flat, preferred_element_type=jnp.float32).astype(jnp.bfloat16)
        return out.reshape(SUB, SUB, dim)

    def bytes_of_all(ref, c, sem):
        view = ref.at[pl.ds(0, n_tab - tabs), pl.ds(c * part, part), :]
        return pltpu.make_async_copy(view, view, sem)

    for c in range(n_chunk):
        bytes_of_all(got, c, f_recv.at[c]).wait()
        kept = got.at[pl.ds(me * tabs, tabs), pl.ds(c * part, part), :]
        pltpu.make_async_copy(kept, kept, f_own.at[c]).wait()

        def to_samples(g, carry, c=c):
            first = pl.multiple_of(g * SUB, SUB)
            mine[pl.ds(c * part, part), pl.ds(first, SUB), :] = swap_tile(
                got[pl.ds(first, SUB), pl.ds(c * part, part), :]
            )
            return carry

        lax.fori_loop(0, groups, to_samples, 0, unroll=2)

        def sample(i, carry, c=c):
            for u in range(4):
                b = c * part + i * 4 + u
                vectors = mine[b]
                inter_ref[0, b] = lax.dot_general(
                    vectors, vectors, (((1,), (1,)), ((), ())), preferred_element_type=jnp.float32
                ).astype(jnp.bfloat16)
                cot = cot_ref[0, b]
                both = jnp.concatenate([cot, cot.T], axis=1)
                dmine[b] = jnp.dot(
                    both,
                    jnp.concatenate([vectors, vectors], axis=0),
                    preferred_element_type=jnp.float32,
                ).astype(jnp.bfloat16)
            return carry

        lax.fori_loop(0, part // 4, sample, 0)

        def to_tables(i, carry, c=c):
            away = lax.rem(i, 2) * ((i + 1) // 2) + (1 - lax.rem(i, 2)) * (groups - i // 2)
            g = lax.rem(me // per_group + away, groups)
            first = pl.multiple_of(g * SUB, SUB)
            dsend[pl.ds(first, SUB), pl.ds(c * part, part), :] = swap_tile(
                dmine[pl.ds(c * part, part), pl.ds(first, SUB), :]
            )
            for q in range(per_group):
                dest = g * per_group + lax.rem(me + q, per_group)
                src = dsend.at[pl.ds(dest * tabs, tabs), pl.ds(c * part, part), :]
                dst = dgot.at[:, pl.ds(me * own + c * part, part), :]

                @pl.when(dest == me)
                def _():
                    pltpu.make_async_copy(src, dst, b_own.at[c]).start()

                @pl.when(dest != me)
                def _():
                    pltpu.make_async_remote_copy(
                        src_ref=src,
                        dst_ref=dst,
                        send_sem=b_send.at[c],
                        recv_sem=b_recv.at[c],
                        device_id={"shard": dest},
                        device_id_type=MESH,
                    ).start()

            return carry

        lax.fori_loop(0, groups, to_tables, 0)

    for c in range(n_chunk):
        bytes_of_all(got, c, b_recv.at[c]).wait()
        kept = got.at[pl.ds(me * tabs, tabs), pl.ds(c * part, part), :]
        pltpu.make_async_copy(kept, kept, b_own.at[c]).wait()

    for t in range(tabs):

        def grad(i, carry, t=t):
            first = pl.multiple_of(i * 256, 256)
            value = jnp.dot(
                counts[t, pl.ds(first, 256), :], dgot[t], preferred_element_type=jnp.float32
            )
            partial[t, pl.ds(first, 256), :] = value
            part_low[t, pl.ds(first, 256), :] = value.astype(jnp.bfloat16)
            return carry

        lax.fori_loop(0, width // 256, grad, 0)

    half = pltpu.make_async_remote_copy(
        src_ref=part_low.at[1 - core],
        dst_ref=half_got,
        send_sem=c_send,
        recv_sem=c_recv,
        device_id={"rep": sibling},
        device_id_type=MESH,
    )
    half.start()
    half.wait()
    total = partial[core] + half_got[...].astype(jnp.float32)
    partial[core] = total
    half_low[...] = total.astype(jnp.bfloat16)

    piece = width // n_y

    def scatter(i, carry):
        peer = lax.rem(y + i, n_y)
        pltpu.make_async_remote_copy(
            src_ref=half_low.at[pl.ds(pl.multiple_of(peer * piece, piece), piece), :],
            dst_ref=y_got.at[y],
            send_sem=y_send,
            recv_sem=y_recv,
            device_id={"rep": peer * CORES + core},
            device_id_type=MESH,
        ).start()
        return carry

    lax.fori_loop(1, n_y, scatter, 0)
    y_got[y] = jnp.zeros((piece, dim), jnp.bfloat16)
    seven = y_got.at[pl.ds(0, n_y - 1)]
    pltpu.make_async_copy(seven, seven, y_recv).wait()
    here = pl.ds(pl.multiple_of(y * piece, piece), piece)
    total = partial[core, here, :]
    for i in range(n_y):
        total = total + y_got[i].astype(jnp.float32)
    sums[core, here, :] = total.astype(jnp.bfloat16)

    def spread(i, carry):
        peer = lax.rem(y + i, n_y)
        pltpu.make_async_remote_copy(
            src_ref=sums.at[core, here, :],
            dst_ref=sums.at[core, here, :],
            send_sem=g_send,
            recv_sem=g_recv,
            device_id={"rep": peer * CORES + core},
            device_id_type=MESH,
        ).start()
        return carry

    lax.fori_loop(1, n_y, spread, 0)
    pltpu.make_async_copy(seven, seven, g_recv).wait()
    last = pltpu.make_async_remote_copy(
        src_ref=sums.at[core],
        dst_ref=other,
        send_sem=h_send,
        recv_sem=h_recv,
        device_id={"rep": sibling},
        device_id_type=MESH,
    )
    last.start()

    def update(t, gradient):
        mean = jnp.sum(gradient * gradient, axis=1, keepdims=True) * (1.0 / dim)
        acc_new = acc_ref[t][:, :1] + mean
        new_ref[t] = rows_ref[t] - learn_rate * gradient / (jnp.sqrt(acc_new) + epsilon)

    update(core, sums[core].astype(jnp.float32))
    last.wait()
    update(1 - core, other[...].astype(jnp.float32))

    for c in range(n_chunk):
        bytes_of_all(got, c, f_send.at[c]).wait()
        bytes_of_all(got, c, b_send.at[c]).wait()
    pltpu.make_async_copy(seven, seven, y_send).wait()
    pltpu.make_async_copy(seven, seven, g_send).wait()


def local(n_shard, n_rep, emb_table, accumulated, touched, bag_slots, lengths, cotangent):
    tabs, width = touched.shape
    dim = emb_table.shape[2]
    batch = bag_slots.shape[2]
    own = batch // n_shard
    n_tab = tabs * n_shard
    n_chunk = own // SUB
    n_y = n_rep // CORES
    rows, acc_rows = gather_rows(emb_table, accumulated, touched)
    slots = jnp.swapaxes(bag_slots[:, 0], 1, 2)
    dma = pltpu.SemaphoreType.DMA
    low = jnp.bfloat16
    return pl.pallas_call(
        functools.partial(main_kernel, n_shard, n_rep, n_chunk),
        out_shape=(
            jax.ShapeDtypeStruct((1, own, n_tab, n_tab), low),
            jax.ShapeDtypeStruct((tabs, width, dim), jnp.float32),
        ),
        in_specs=[VMEM] * 5,
        out_specs=(VMEM, VMEM),
        scratch_shapes=[
            pltpu.VMEM((tabs, width, dim), low),
            pltpu.VMEM((tabs, width, batch), low),
            pltpu.VMEM((tabs, batch, dim), low),
            pltpu.VMEM((n_tab, own, dim), low),
            pltpu.VMEM((own, n_tab, dim), low),
            pltpu.VMEM((own, n_tab, dim), low),
            pltpu.VMEM((n_tab, own, dim), low),
            pltpu.VMEM((tabs, batch, dim), low),
            pltpu.VMEM((tabs, width, dim), jnp.float32),
            pltpu.VMEM((tabs, width, dim), low),
            pltpu.VMEM((width, dim), low),
            pltpu.VMEM((width, dim), low),
            pltpu.VMEM((n_y, width // n_y, dim), low),
            pltpu.VMEM((tabs, width, dim), low),
            pltpu.VMEM((width, dim), low),
            *[dma((n_chunk,))] * 6,
            *[dma] * 8,
        ],
        compiler_params=pltpu.CompilerParams(
            collective_id=0, has_side_effects=True, vmem_limit_bytes=52 << 20
        ),
    )(rows, acc_rows, slots, lengths, cotangent)


def solution(mesh):
    return jax.shard_map(
        functools.partial(local, mesh.shape["shard"], mesh.shape["rep"]),
        mesh=mesh,
        in_specs=(
            P("shard", None, None),
            P("shard", None),
            P("shard", None),
            P("shard", "rep", None, None),
            P("shard", "rep", None),
            P("rep", "shard", None, None),
        ),
        out_specs=(P("rep", "shard", None, None), P("shard", None, None)),
        check_vma=False,
    )
```

```python
import functools

import jax
import jax.numpy as jnp
from jax import lax
from jax.experimental import pallas as pl
from jax.experimental.pallas import tpu as pltpu
from jax.sharding import PartitionSpec as P

MESH = pl.DeviceIdType.MESH
VMEM = pl.BlockSpec(memory_space=pltpu.VMEM)
HBM = pl.BlockSpec(memory_space=pl.ANY)
learn_rate = 0.5
epsilon = 1e-08
LANES = 128
SUB = 16
CORES = 2


def main_kernel(
    n_shard, n_rep, ring, n_chunk,
    table_ref, acc_ref, touched_ref, slot_ref, len_ref, cot_ref,
    inter_ref, new_ref,
    table, acc, touched, slots, cot, inter, rows, acc_rows, low, counts, pooled, got, mine, dmine, dsend, dgot,
    partial, part_low, half_got, half_low, y_got, sums, new,
    in_sem, out_sem, f_send, f_recv, f_own, b_send, b_recv, b_own,
    c_send, c_recv, y_send, y_recv, g_send, g_recv, h_send, h_recv,
):
    me = lax.axis_index("shard")
    rep = lax.axis_index("rep")
    core = lax.rem(rep, CORES)
    y = rep // CORES
    z = me // ring
    x = lax.rem(me, ring)
    n_y = n_rep // CORES
    n_z = n_shard // ring
    tabs, width, dim = rows.shape
    batch = slot_ref.shape[2]
    deep = slot_ref.shape[1]
    own = batch // n_shard
    span = batch // n_chunk
    n_tab = tabs * n_shard
    sibling = rep + 1 - 2 * core

    loads = [
        pltpu.make_async_copy(touched_ref, touched, in_sem.at[0]),
        pltpu.make_async_copy(acc_ref, acc, in_sem.at[1]),
        *[pltpu.make_async_copy(table_ref.at[t], table.at[t], in_sem.at[2 + t]) for t in range(tabs)],
        pltpu.make_async_copy(cot_ref.at[0], cot, in_sem.at[2 + tabs]),
    ]
    for load in loads:
        load.start()

    barrier = pltpu.get_barrier_semaphore()

    def greet(i, carry):
        pl.semaphore_signal(
            barrier, inc=1, device_id={"shard": lax.rem(me + i, n_shard)}, device_id_type=MESH
        )
        return carry

    lax.fori_loop(1, n_shard, greet, 0)

    def greet_y(i, carry):
        peer = lax.rem(y + i, n_y) * CORES + core
        pl.semaphore_signal(barrier, inc=1, device_id={"rep": peer}, device_id_type=MESH)
        return carry

    lax.fori_loop(1, n_y, greet_y, 0)
    pl.semaphore_signal(barrier, inc=1, device_id={"rep": sibling}, device_id_type=MESH)

    wide = own * ring
    line = wide // n_chunk
    from_lane = lax.broadcasted_iota(jnp.int32, (wide, wide), 0)
    to_lane = lax.broadcasted_iota(jnp.int32, (wide, wide), 1)
    home = lax.rem(to_lane, line) // SUB * own + to_lane // line * SUB + lax.rem(to_lane, SUB)
    sort = jnp.where(from_lane == home, 1.0, 0.0).astype(jnp.bfloat16)

    def sort_slots(r, carry):
        first = pl.multiple_of(r * wide, wide)
        halves = []
        for t in range(tabs):
            ids = slot_ref[t, :, pl.ds(first, wide)]
            sizes = len_ref[t, :, pl.ds(first, wide)]
            place = lax.broadcasted_iota(jnp.int32, ids.shape, 0)
            ids = jnp.where(place < sizes, ids, -1)
            halves += [ids & 255, ids >> 8]
        stack = jnp.concatenate(halves, axis=0).astype(jnp.float32).astype(jnp.bfloat16)
        moved = jnp.dot(stack, sort, preferred_element_type=jnp.float32)
        for t in range(tabs):
            lo = moved[2 * t * deep : (2 * t + 1) * deep]
            hi = moved[(2 * t + 1) * deep : (2 * t + 2) * deep]
            ids = (lo + 256.0 * hi).astype(jnp.int32)
            for c in range(n_chunk):
                slots[t, :, pl.ds(pl.multiple_of(c * span + r * line, line), line)] = ids[
                    :, c * line : (c + 1) * line
                ]
        return carry

    lax.fori_loop(0, n_z, sort_slots, 0)

    key0 = lax.broadcasted_iota(jnp.int32, (SUB, LANES), 0)
    one = jnp.ones((SUB, LANES), jnp.bfloat16)
    zero = jnp.zeros((SUB, LANES), jnp.bfloat16)

    def count(t, first):
        ids = slots[t, :, pl.ds(first, LANES)]
        each = [
            jnp.broadcast_to(ids[l : l + 1], (SUB, LANES)).astype(jnp.int16) for l in range(deep)
        ]
        for tile in range(width // SUB):
            key = (key0 + tile * SUB).astype(jnp.int16)
            terms = [jnp.where(key == e, one, zero) for e in each]
            while len(terms) > 1:
                terms = [a + b for a, b in zip(terms[::2], terms[1::2])]
            counts[t, pl.ds(tile * SUB, SUB), pl.ds(first, LANES)] = terms[0]

    def pool(t, first):
        pooled[t, pl.ds(first, LANES), :] = lax.dot_general(
            counts[t, :, pl.ds(first, LANES)],
            low[t],
            (((0,), (0,)), ((), ())),
            preferred_element_type=jnp.float32,
        ).astype(jnp.bfloat16)

    for load in (loads[0], *loads[2 : 2 + tabs]):
        load.wait()
    gathered = width // n_z

    def count_and_gather(r, carry):
        for t in range(tabs):
            for g in range(gathered // SUB):
                base = pl.multiple_of(r * gathered + g * SUB, SUB)
                picked = jnp.concatenate(
                    [
                        table[t, pl.ds(touched[t, r * gathered + g * SUB + u], 1), :]
                        for u in range(SUB)
                    ],
                    axis=0,
                )
                rows[t, pl.ds(base, SUB), :] = picked
                low[t, pl.ds(base, SUB), :] = picked.astype(jnp.bfloat16)
            count(t, pl.multiple_of(r * line, line))
        return carry

    lax.fori_loop(0, n_z, count_and_gather, 0)
    pl.semaphore_wait(barrier, n_shard - 1 + n_y - 1 + 1)

    def z_pair(i):
        away = lax.rem(i, 2) * ((i + 1) // 2) + (1 - lax.rem(i, 2)) * (n_z - i // 2)
        near = lax.rem(z + away, n_z)
        return near, lax.rem(near + n_z // 2, n_z)

    def send(src, dst, dest, sent, landed, kept):
        @pl.when(dest == me)
        def _():
            pltpu.make_async_copy(src, dst, kept).start()

        @pl.when(dest != me)
        def _():
            pltpu.make_async_remote_copy(
                src_ref=src,
                dst_ref=dst,
                send_sem=sent,
                recv_sem=landed,
                device_id={"shard": dest},
                device_id_type=MESH,
            ).start()

    def forward(i, carry, c):
        pair = z_pair(i)
        for r in pair:
            first = pl.multiple_of(c * span + r * line, line)
            for t in range(tabs):
                if c > 0:
                    count(t, first)
                pool(t, first)

        def out(q, carry):
            for r, column in zip(pair, (lax.rem(x + q, ring), lax.rem(x + ring - q, ring))):
                dest = r * ring + column
                send(
                    pooled.at[:, pl.ds(c * span + dest * SUB, SUB), :],
                    got.at[pl.ds(me * tabs, tabs), pl.ds(c * SUB, SUB), :],
                    dest,
                    f_send.at[c],
                    f_recv.at[c],
                    f_own.at[c],
                )
            return carry

        return lax.fori_loop(0, ring, out, carry)

    for c in range(n_chunk):
        lax.fori_loop(0, n_z // 2, functools.partial(forward, c=c), 0)

    loads[1].wait()

    def gather_acc(i, carry):
        for t in range(tabs):
            base = pl.multiple_of(i * 8, 8)
            acc_rows[t, pl.ds(base, 8), :] = jnp.concatenate(
                [
                    jnp.full((1, LANES), acc[t, touched[t, i * 8 + u]], jnp.float32)
                    for u in range(8)
                ],
                axis=0,
            )
        return carry

    lax.fori_loop(0, width // 8, gather_acc, 0)
    loads[2 + tabs].wait()

    swap_row = lax.broadcasted_iota(jnp.int32, (SUB * SUB, SUB * SUB), 0)
    swap_col = lax.broadcasted_iota(jnp.int32, (SUB * SUB, SUB * SUB), 1)
    swapped = lax.rem(swap_col, SUB) * SUB + swap_col // SUB
    swap = jnp.where(swap_row == swapped, 1.0, 0.0).astype(jnp.bfloat16)

    def swap_tile(tile):
        flat = tile.reshape(SUB * SUB, dim)
        out = jnp.dot(swap, flat, preferred_element_type=jnp.float32).astype(jnp.bfloat16)
        return out.reshape(SUB, SUB, dim)

    def all_of(ref, t0, count_t, sem):
        view = ref.at[pl.ds(t0, count_t), pl.ds(0, (n_shard - 1) * SUB), :]
        return pltpu.make_async_copy(view, view, sem)

    def own_of(t0, count_t, sem):
        view = pooled.at[pl.ds(t0, count_t), pl.ds(0, SUB), :]
        return pltpu.make_async_copy(view, view, sem)

    per_group = SUB // tabs
    for c in range(n_chunk):
        all_of(pooled, 0, tabs, f_recv.at[c]).wait()
        own_of(0, tabs, f_own.at[c]).wait()
        part = pl.ds(c * SUB, SUB)

        def to_samples(g, carry, part=part):
            first = pl.multiple_of(g * SUB, SUB)
            mine[part, pl.ds(first, SUB), :] = swap_tile(got[pl.ds(first, SUB), part, :])
            return carry

        lax.fori_loop(0, n_tab // SUB, to_samples, 0, unroll=2)

        def sample(i, carry, c=c):
            for u in range(4):
                b = c * SUB + i * 4 + u
                vectors = mine[b]
                inter[b] = lax.dot_general(
                    vectors, vectors, (((1,), (1,)), ((), ())), preferred_element_type=jnp.float32
                ).astype(jnp.bfloat16)
                both = jnp.concatenate([cot[b], cot[b].T], axis=1)
                dmine[b] = jnp.dot(
                    both,
                    jnp.concatenate([vectors, vectors], axis=0),
                    preferred_element_type=jnp.float32,
                ).astype(jnp.bfloat16)
            return carry

        lax.fori_loop(0, SUB // 4, sample, 0)
        pltpu.make_async_copy(inter.at[part], inter_ref.at[0, part], out_sem.at[c]).start()

        split = [(0, tabs)] if c < n_chunk - 1 else [(t, 1) for t in range(tabs)]

        def to_tables(i, carry, part=part):
            for g in z_pair(i):
                first = pl.multiple_of(g * SUB, SUB)
                dsend[pl.ds(first, SUB), part, :] = swap_tile(dmine[part, pl.ds(first, SUB), :])
            return carry

        def backward(i, carry, c, k, t0, count_t):
            def out(q, carry):
                columns = (lax.rem(x + q, ring), lax.rem(x + ring - q, ring))
                for r, column in zip(z_pair(i), columns):
                    dest = r * ring + column
                    send(
                        dsend.at[pl.ds(dest * tabs + t0, count_t), pl.ds(c * SUB, SUB), :],
                        dgot.at[pl.ds(t0, count_t), pl.ds(c * span + me * SUB, SUB), :],
                        dest,
                        b_send.at[k],
                        b_recv.at[k],
                        b_own.at[k],
                    )
                return carry

            return lax.fori_loop(0, ring, out, carry)

        for j, (t0, count_t) in enumerate(split):

            def turn(i, carry, c=c, j=j, t0=t0, count_t=count_t):
                if j == 0:
                    to_tables(i, carry)
                return backward(i, carry, c, c + j, t0, count_t)

            lax.fori_loop(0, n_z // 2, turn, 0)

    def gradient(t, c):
        def rows_of(i, carry):
            first = pl.multiple_of(i * 256, 256)
            value = jnp.dot(
                counts[t, pl.ds(first, 256), pl.ds(c * span, span)],
                dgot[t, pl.ds(c * span, span), :],
                preferred_element_type=jnp.float32,
            )
            if c > 0:
                value = value + partial[t, pl.ds(first, 256), :]
            partial[t, pl.ds(first, 256), :] = value
            if c == n_chunk - 1:
                part_low[t, pl.ds(first, 256), :] = value.astype(jnp.bfloat16)
            return carry

        lax.fori_loop(0, width // 256, rows_of, 0)

    for c in range(n_chunk - 1):
        all_of(pooled, 0, tabs, b_recv.at[c]).wait()
        own_of(0, tabs, b_own.at[c]).wait()
        for t in range(tabs):
            gradient(t, c)

    half = width // CORES
    piece = half // n_y
    kept = pl.ds(pl.multiple_of(core * half, half), half)
    given = pl.ds(pl.multiple_of((1 - core) * half, half), half)
    here = pl.ds(pl.multiple_of(core * half + y * piece, piece), piece)
    last = n_chunk - 1
    ends = []
    for t in range(tabs):
        all_of(pooled, t, 1, b_recv.at[last + t]).wait()
        own_of(t, 1, b_own.at[last + t]).wait()
        gradient(t, last)
        trade = pltpu.make_async_remote_copy(
            src_ref=part_low.at[t, given, :],
            dst_ref=half_got.at[t],
            send_sem=c_send.at[t],
            recv_sem=c_recv.at[t],
            device_id={"rep": sibling},
            device_id_type=MESH,
        )
        trade.start()
        trade.wait()
        total = partial[t, kept, :] + half_got[t].astype(jnp.float32)
        partial[t, kept, :] = total
        half_low[t] = total.astype(jnp.bfloat16)

        def scatter(i, carry, t=t):
            peer = lax.rem(y + i, n_y)
            pltpu.make_async_remote_copy(
                src_ref=half_low.at[t, pl.ds(pl.multiple_of(peer * piece, piece), piece), :],
                dst_ref=y_got.at[t, y],
                send_sem=y_send.at[t],
                recv_sem=y_recv.at[t],
                device_id={"rep": peer * CORES + core},
                device_id_type=MESH,
            ).start()
            return carry

        lax.fori_loop(1, n_y, scatter, 0)
        y_got[t, y] = jnp.zeros((piece, dim), jnp.bfloat16)
        others = y_got.at[t, pl.ds(0, n_y - 1)]
        pltpu.make_async_copy(others, others, y_recv.at[t]).wait()
        total = partial[t, here, :]
        for i in range(n_y):
            total = total + y_got[t, i].astype(jnp.float32)
        sums[t, here, :] = total.astype(jnp.bfloat16)

        def spread(i, carry, t=t):
            peer = lax.rem(y + i, n_y)
            pltpu.make_async_remote_copy(
                src_ref=sums.at[t, here, :],
                dst_ref=sums.at[t, here, :],
                send_sem=g_send.at[t],
                recv_sem=g_recv.at[t],
                device_id={"rep": peer * CORES + core},
                device_id_type=MESH,
            ).start()
            return carry

        lax.fori_loop(1, n_y, spread, 0)
        pltpu.make_async_copy(others, others, g_recv.at[t]).wait()
        end = pltpu.make_async_remote_copy(
            src_ref=sums.at[t, kept, :],
            dst_ref=sums.at[t, kept, :],
            send_sem=h_send.at[t],
            recv_sem=h_recv.at[t],
            device_id={"rep": sibling},
            device_id_type=MESH,
        )
        end.start()
        end.wait()
        summed = sums[t].astype(jnp.float32)
        mean = jnp.sum(summed * summed, axis=1, keepdims=True) * (1.0 / dim)
        scale = learn_rate / (jnp.sqrt(acc_rows[t][:, :1] + mean) + epsilon)
        new[t] = rows[t] - summed * scale
        out = pltpu.make_async_copy(new.at[t], new_ref.at[t], out_sem.at[n_chunk + t])
        out.start()
        ends.append(out)

    for c in range(n_chunk):
        all_of(pooled, 0, tabs, f_send.at[c]).wait()
        part = pl.ds(c * SUB, SUB)
        pltpu.make_async_copy(inter.at[part], inter_ref.at[0, part], out_sem.at[c]).wait()
    for c in range(n_chunk - 1):
        all_of(pooled, 0, tabs, b_send.at[c]).wait()
    for t in range(tabs):
        all_of(pooled, t, 1, b_send.at[last + t]).wait()
        others = y_got.at[t, pl.ds(0, n_y - 1)]
        pltpu.make_async_copy(others, others, y_send.at[t]).wait()
        pltpu.make_async_copy(others, others, g_send.at[t]).wait()
        ends[t].wait()


def local(n_shard, n_rep, emb_table, accumulated, touched, bag_slots, lengths, cotangent):
    tabs, width = touched.shape
    size, dim = emb_table.shape[1:]
    batch = bag_slots.shape[2]
    own = batch // n_shard
    n_tab = tabs * n_shard
    n_chunk = own // SUB
    n_y = n_rep // CORES
    ring = SUB // tabs
    half = width // CORES
    slots = jnp.swapaxes(bag_slots[:, 0], 1, 2)
    dma = pltpu.SemaphoreType.DMA
    low = jnp.bfloat16
    f32 = jnp.float32
    return pl.pallas_call(
        functools.partial(main_kernel, n_shard, n_rep, ring, n_chunk),
        out_shape=(
            jax.ShapeDtypeStruct((1, own, n_tab, n_tab), low),
            jax.ShapeDtypeStruct((tabs, width, dim), f32),
        ),
        in_specs=[HBM, HBM, HBM, VMEM, VMEM, HBM],
        out_specs=(HBM, HBM),
        scratch_shapes=[
            pltpu.VMEM((tabs, size, dim), f32),
            pltpu.SMEM((tabs, size), f32),
            pltpu.SMEM((tabs, width), jnp.int32),
            pltpu.VMEM(slots.shape, jnp.int32),
            pltpu.VMEM((own, n_tab, n_tab), low),
            pltpu.VMEM((own, n_tab, n_tab), low),
            pltpu.VMEM((tabs, width, dim), f32),
            pltpu.VMEM((tabs, width, LANES), f32),
            pltpu.VMEM((tabs, width, dim), low),
            pltpu.VMEM((tabs, width, batch), low),
            pltpu.VMEM((tabs, batch, dim), low),
            pltpu.VMEM((n_tab, own, dim), low),
            pltpu.VMEM((own, n_tab, dim), low),
            pltpu.VMEM((own, n_tab, dim), low),
            pltpu.VMEM((n_tab, own, dim), low),
            pltpu.VMEM((tabs, batch, dim), low),
            pltpu.VMEM((tabs, width, dim), f32),
            pltpu.VMEM((tabs, width, dim), low),
            pltpu.VMEM((tabs, half, dim), low),
            pltpu.VMEM((tabs, half, dim), low),
            pltpu.VMEM((tabs, n_y, half // n_y, dim), low),
            pltpu.VMEM((tabs, width, dim), low),
            pltpu.VMEM((tabs, width, dim), f32),
            dma((3 + tabs,)),
            dma((n_chunk + tabs,)),
            *[dma((n_chunk,))] * 3,
            *[dma((n_chunk - 1 + tabs,))] * 3,
            *[dma((tabs,))] * 8,
        ],
        compiler_params=pltpu.CompilerParams(
            collective_id=0, has_side_effects=True, vmem_limit_bytes=56 << 20
        ),
    )(emb_table, accumulated, touched, slots, lengths, cotangent)


def solution(mesh):
    return jax.shard_map(
        functools.partial(local, mesh.shape["shard"], mesh.shape["rep"]),
        mesh=mesh,
        in_specs=(
            P("shard", None, None),
            P("shard", None),
            P("shard", None),
            P("shard", "rep", None, None),
            P("shard", "rep", None),
            P("rep", "shard", None, None),
        ),
        out_specs=(P("rep", "shard", None, None), P("shard", None, None)),
        check_vma=False,
    )
```

```python
import functools

import jax
import jax.numpy as jnp
from jax import lax
from jax.experimental import pallas as pl
from jax.experimental.pallas import tpu as pltpu
from jax.sharding import PartitionSpec as P

MESH = pl.DeviceIdType.MESH
VMEM = pl.BlockSpec(memory_space=pltpu.VMEM)
HBM = pl.BlockSpec(memory_space=pl.ANY)
learn_rate = 0.5
epsilon = 1e-08
LANES = 128
SUB = 16
CORES = 2


def main_kernel(
    n_shard, n_rep, ring, n_chunk,
    table_ref, acc_ref, touched_ref, slot_ref, len_ref, cot_ref,
    inter_ref, new_ref,
    table, acc, touched, slots, cot, inter, rows, acc_rows, low, counts, pooled, got, mine, dmine, dsend, dgot,
    partial, part_low, half_got, half_low, y_got, sums, new,
    slots_out, slots_far, low_far, counts_far, pooled_far, dfar,
    far_low, far_half, far_kept, far_half_low, far_y, far_out, far_in,
    in_sem, out_sem, f_send, f_recv, f_own, b_send, b_recv, b_own,
    c_send, c_recv, y_send, y_recv, g_send, g_recv, h_send, h_recv,
    e_send, e_recv, e_own, s_send, s_recv, r_send, r_recv, w_send, w_recv, v_send, v_recv,
    i_send, i_recv, j_send, j_recv, k_send, k_recv,
):
    me = lax.axis_index("shard")
    rep = lax.axis_index("rep")
    core = lax.rem(rep, CORES)
    y = rep // CORES
    z = me // ring
    x = lax.rem(me, ring)
    n_y = n_rep // CORES
    n_z = n_shard // ring
    tabs, width, dim = rows.shape
    batch = slot_ref.shape[2]
    deep = slot_ref.shape[1]
    own = batch // n_shard
    span = batch // n_chunk
    n_tab = tabs * n_shard
    sibling = rep + 1 - 2 * core
    turn = 1 - 2 * core
    opposite = lax.rem(z + n_z // 2, n_z) * ring + lax.rem(x + ring // 2, ring)
    near_x = (0, 1, -1, 2)
    far_x = (4, 5, 3, 6)
    dgot[...] = jnp.zeros_like(dgot)
    dfar[...] = jnp.zeros_like(dfar)

    loads = [
        pltpu.make_async_copy(touched_ref, touched, in_sem.at[0]),
        pltpu.make_async_copy(acc_ref, acc, in_sem.at[1]),
        *[pltpu.make_async_copy(table_ref.at[t], table.at[t], in_sem.at[2 + t]) for t in range(tabs)],
        pltpu.make_async_copy(cot_ref.at[0], cot, in_sem.at[2 + tabs]),
    ]
    for load in loads:
        load.start()

    barrier = pltpu.get_barrier_semaphore()

    def greet(i, carry):
        pl.semaphore_signal(
            barrier, inc=1, device_id={"shard": lax.rem(me + i, n_shard)}, device_id_type=MESH
        )
        return carry

    lax.fori_loop(1, n_shard, greet, 0)

    def greet_y(i, carry):
        peer = lax.rem(y + i, n_y) * CORES + core
        pl.semaphore_signal(barrier, inc=1, device_id={"rep": peer}, device_id_type=MESH)
        return carry

    lax.fori_loop(1, n_y, greet_y, 0)
    pl.semaphore_signal(barrier, inc=1, device_id={"rep": sibling}, device_id_type=MESH)

    wide = own * ring
    line = wide // n_chunk
    from_lane = lax.broadcasted_iota(jnp.int32, (wide, wide), 0)
    to_lane = lax.broadcasted_iota(jnp.int32, (wide, wide), 1)
    home = lax.rem(to_lane, line) // SUB * own + to_lane // line * SUB + lax.rem(to_lane, SUB)
    sort = jnp.where(from_lane == home, 1.0, 0.0).astype(jnp.bfloat16)

    def sort_slots(r, carry):
        first = pl.multiple_of(r * wide, wide)
        halves = []
        for t in range(tabs):
            ids = slot_ref[t, :, pl.ds(first, wide)]
            sizes = len_ref[t, :, pl.ds(first, wide)]
            place = lax.broadcasted_iota(jnp.int32, ids.shape, 0)
            ids = jnp.where(place < sizes, ids, -1)
            halves += [ids & 255, ids >> 8]
        stack = jnp.concatenate(halves, axis=0).astype(jnp.float32).astype(jnp.bfloat16)
        moved = jnp.dot(stack, sort, preferred_element_type=jnp.float32)
        for t in range(tabs):
            lo = moved[2 * t * deep : (2 * t + 1) * deep]
            hi = moved[(2 * t + 1) * deep : (2 * t + 2) * deep]
            ids = (lo + 256.0 * hi).astype(jnp.int32)
            for c in range(n_chunk):
                lanes = pl.ds(pl.multiple_of(c * span + r * line, line), line)
                slots[t, :, lanes] = ids[:, c * line : (c + 1) * line]
                slots_out[pl.ds(t * deep, deep), lanes] = ids[:, c * line : (c + 1) * line].astype(
                    jnp.int16
                )
        return carry

    lax.fori_loop(0, n_z, sort_slots, 0)

    key0 = lax.broadcasted_iota(jnp.int32, (SUB, LANES), 0)
    one = jnp.ones((SUB, LANES), jnp.bfloat16)
    zero = jnp.zeros((SUB, LANES), jnp.bfloat16)

    def count(ids, t, to, first):
        each = [
            jnp.broadcast_to(ids[l : l + 1], (SUB, LANES)).astype(jnp.int16) for l in range(deep)
        ]
        for tile in range(width // SUB):
            key = (key0 + tile * SUB).astype(jnp.int16)
            terms = [jnp.where(key == e, one, zero) for e in each]
            while len(terms) > 1:
                terms = [a + b for a, b in zip(terms[::2], terms[1::2])]
            to[t, pl.ds(tile * SUB, SUB), pl.ds(first, LANES)] = terms[0]

    def count_own(t, first):
        count(slots[t, :, pl.ds(first, LANES)], t, counts, first)

    def pool(t, first, made, weights, to):
        to[t, pl.ds(first, LANES), :] = lax.dot_general(
            made[t, :, pl.ds(first, LANES)],
            weights[t],
            (((0,), (0,)), ((), ())),
            preferred_element_type=jnp.float32,
        ).astype(jnp.bfloat16)

    for load in (loads[0], *loads[2 : 2 + tabs]):
        load.wait()
    gathered = width // n_z

    def count_and_gather(r, carry):
        for t in range(tabs):
            for g in range(gathered // SUB):
                base = pl.multiple_of(r * gathered + g * SUB, SUB)
                picked = jnp.concatenate(
                    [
                        table[t, pl.ds(touched[t, r * gathered + g * SUB + u], 1), :]
                        for u in range(SUB)
                    ],
                    axis=0,
                )
                rows[t, pl.ds(base, SUB), :] = picked
                low[t, pl.ds(base, SUB), :] = picked.astype(jnp.bfloat16)
            count_own(t, pl.multiple_of(r * line, line))
        return carry

    lax.fori_loop(0, n_z, count_and_gather, 0)
    pl.semaphore_wait(barrier, n_shard - 1 + n_y - 1 + 1)

    def z_pair(i, way):
        away = lax.rem(i, 2) * ((i + 1) // 2) + (1 - lax.rem(i, 2)) * (n_z - i // 2)
        near = lax.rem(z + way * away + 2 * n_z, n_z)
        return near, lax.rem(near + n_z // 2, n_z)

    def x_at(away, way):
        return lax.rem(x + way * away + 2 * ring, ring)

    share = width // n_y
    lent = pl.ds(pl.multiple_of(y * share, share), share)
    lend_rows = pltpu.make_async_remote_copy(
        src_ref=low.at[core, lent, :],
        dst_ref=low_far.at[core, lent, :],
        send_sem=r_send,
        recv_sem=r_recv,
        device_id={"shard": opposite},
        device_id_type=MESH,
    )
    lend_rows.start()

    def lend_slots(i, carry):
        far = z_pair(i, turn)[1]
        for c in range(n_chunk):
            lanes = pl.ds(pl.multiple_of(c * span + far * line, line), line)
            pltpu.make_async_remote_copy(
                src_ref=slots_out.at[:, lanes],
                dst_ref=slots_far.at[:, lanes],
                send_sem=s_send,
                recv_sem=s_recv,
                device_id={"shard": opposite},
                device_id_type=MESH,
            ).start()
        return carry

    lax.fori_loop(0, n_z // 2, lend_slots, 0)

    def send(src, dst, dest, sent, landed, kept):
        @pl.when(dest == me)
        def _():
            pltpu.make_async_copy(src, dst, kept).start()

        @pl.when(dest != me)
        def _():
            pltpu.make_async_remote_copy(
                src_ref=src,
                dst_ref=dst,
                send_sem=sent,
                recv_sem=landed,
                device_id={"shard": dest},
                device_id_type=MESH,
            ).start()

    def forward(i, carry, c):
        pair = z_pair(i, turn)
        for r in pair:
            for t in range(tabs):
                pool(t, pl.multiple_of(c * span + r * line, line), counts, low, pooled)

        def out(r, column):
            dest = r * ring + column
            send(
                pooled.at[:, pl.ds(c * span + dest * SUB, SUB), :],
                got.at[pl.ds(me * tabs, tabs), pl.ds(c * SUB, SUB), :],
                dest,
                f_send.at[c],
                f_recv.at[c],
                f_own.at[c],
            )

        for j in range(ring // 2):
            out(pair[0], x_at(near_x[j], turn))
            out(pair[1], x_at(-near_x[j], -turn))
            out(pair[0], x_at(far_x[j], turn))
        return carry

    def forward_far(i, carry, c):
        near, far = z_pair(i, turn)
        first = pl.multiple_of(c * span + far * line, line)
        for t in range(tabs):
            ids = slots_far[pl.ds(t * deep, deep), pl.ds(c * span + near * line, line)]
            ids = pltpu.roll(ids.astype(jnp.int32), line // 2, 1)
            count(ids, t, counts_far, first)
            pool(t, first, counts_far, low_far, pooled_far)
        for j in range(ring // 2):
            column = x_at(far_x[j], turn)
            send(
                pooled_far.at[:, pl.ds(c * span + (far * ring + column) * SUB, SUB), :],
                got.at[pl.ds(opposite * tabs, tabs), pl.ds(c * SUB, SUB), :],
                near * ring + lax.rem(column + ring // 2, ring),
                f_send.at[c],
                f_recv.at[c],
                f_own.at[c],
            )
        return carry

    def count_later(r, carry, c):
        for t in range(tabs):
            count_own(t, pl.multiple_of(c * span + r * line, line))
        return carry

    lax.fori_loop(0, n_z // 2, functools.partial(forward, c=0), 0)
    lax.fori_loop(0, n_z // 2, functools.partial(count_later, c=1), 0)
    lend_rows.wait_recv()

    def lend_y(i, carry):
        peer = lax.rem(y + i, n_y)
        pltpu.make_async_remote_copy(
            src_ref=low_far.at[core, lent, :],
            dst_ref=low_far.at[core, lent, :],
            send_sem=w_send,
            recv_sem=w_recv,
            device_id={"rep": peer * CORES + core},
            device_id_type=MESH,
        ).start()
        return carry

    lax.fori_loop(1, n_y, lend_y, 0)
    lax.fori_loop(n_z // 2, n_z, functools.partial(count_later, c=1), 0)
    shares = low_far.at[0, pl.ds(0, (n_y - 1) * share), :]
    pltpu.make_async_copy(shares, shares, w_recv).wait()
    lend_core = pltpu.make_async_remote_copy(
        src_ref=low_far.at[core],
        dst_ref=low_far.at[core],
        send_sem=v_send,
        recv_sem=v_recv,
        device_id={"rep": sibling},
        device_id_type=MESH,
    )
    lend_core.start()
    lines = slots_out.at[:, pl.ds(0, n_chunk * line * (n_z // 2))]
    pltpu.make_async_copy(lines, lines, s_recv).wait()
    lend_core.wait_recv()
    lax.fori_loop(0, n_z // 2, functools.partial(forward_far, c=0), 0)
    lax.fori_loop(0, n_z // 2, functools.partial(forward, c=1), 0)
    lax.fori_loop(0, n_z // 2, functools.partial(forward_far, c=1), 0)

    loads[1].wait()

    def gather_acc(i, carry):
        for t in range(tabs):
            base = pl.multiple_of(i * 8, 8)
            acc_rows[t, pl.ds(base, 8), :] = jnp.concatenate(
                [
                    jnp.full((1, LANES), acc[t, touched[t, i * 8 + u]], jnp.float32)
                    for u in range(8)
                ],
                axis=0,
            )
        return carry

    lax.fori_loop(0, width // 8, gather_acc, 0)
    loads[2 + tabs].wait()

    swap_row = lax.broadcasted_iota(jnp.int32, (SUB * SUB, SUB * SUB), 0)
    swap_col = lax.broadcasted_iota(jnp.int32, (SUB * SUB, SUB * SUB), 1)
    swapped = lax.rem(swap_col, SUB) * SUB + swap_col // SUB
    swap = jnp.where(swap_row == swapped, 1.0, 0.0).astype(jnp.bfloat16)

    def swap_tile(tile):
        flat = tile.reshape(SUB * SUB, dim)
        out = jnp.dot(swap, flat, preferred_element_type=jnp.float32).astype(jnp.bfloat16)
        return out.reshape(SUB, SUB, dim)

    def bytes_of(devices, t0, count_t, sem):
        view = pooled.at[pl.ds(t0, count_t), pl.ds(0, devices * SUB), :]
        return pltpu.make_async_copy(view, view, sem)

    near_both = (n_z // 2) * (ring // 2)
    direct = n_shard - near_both
    for c in range(n_chunk):
        bytes_of(n_shard - 2, 0, tabs, f_recv.at[c]).wait()
        bytes_of(2, 0, tabs, f_own.at[c]).wait()
        part = pl.ds(c * SUB, SUB)

        def to_samples(g, carry, part=part):
            first = pl.multiple_of(g * SUB, SUB)
            mine[part, pl.ds(first, SUB), :] = swap_tile(got[pl.ds(first, SUB), part, :])
            return carry

        lax.fori_loop(0, n_tab // SUB, to_samples, 0, unroll=2)

        def sample(i, carry, c=c):
            for u in range(4):
                b = c * SUB + i * 4 + u
                vectors = mine[b]
                inter[b] = lax.dot_general(
                    vectors, vectors, (((1,), (1,)), ((), ())), preferred_element_type=jnp.float32
                ).astype(jnp.bfloat16)
                both = jnp.concatenate([cot[b], cot[b].T], axis=1)
                dmine[b] = jnp.dot(
                    both,
                    jnp.concatenate([vectors, vectors], axis=0),
                    preferred_element_type=jnp.float32,
                ).astype(jnp.bfloat16)
            return carry

        lax.fori_loop(0, SUB // 4, sample, 0)
        pltpu.make_async_copy(inter.at[part], inter_ref.at[0, part], out_sem.at[c]).start()

        split = [(0, tabs)] if c < n_chunk - 1 else [(t, 1) for t in range(tabs)]

        def to_tables(g, carry, part=part):
            first = pl.multiple_of(g * SUB, SUB)
            dsend[pl.ds(first, SUB), part, :] = swap_tile(dmine[part, pl.ds(first, SUB), :])
            return carry

        lax.fori_loop(0, n_tab // SUB, to_tables, 0, unroll=2)

        def backward_far(i, carry, c=c):
            near, far = z_pair(i, -turn)
            for j in range(ring // 2):
                column = x_at(far_x[j], -turn)
                send(
                    dsend.at[pl.ds((far * ring + column) * tabs, tabs), pl.ds(c * SUB, SUB), :],
                    dfar.at[:, pl.ds(c * span + opposite * SUB, SUB), :],
                    near * ring + lax.rem(column + ring // 2, ring),
                    e_send.at[c],
                    e_recv.at[c],
                    e_own.at[c],
                )
            return carry

        lax.fori_loop(0, n_z // 2, backward_far, 0)

        for j, (t0, count_t) in enumerate(split):

            def backward(i, carry, c=c, k=c + j, t0=t0, count_t=count_t):
                pair = z_pair(i, -turn)

                def out(r, column):
                    dest = r * ring + column
                    send(
                        dsend.at[pl.ds(dest * tabs + t0, count_t), pl.ds(c * SUB, SUB), :],
                        dgot.at[pl.ds(t0, count_t), pl.ds(c * span + me * SUB, SUB), :],
                        dest,
                        b_send.at[k],
                        b_recv.at[k],
                        b_own.at[k],
                    )

                for u in range(ring // 2):
                    out(pair[0], x_at(near_x[u], -turn))
                    out(pair[1], x_at(-near_x[u], turn))
                    out(pair[0], x_at(far_x[u], -turn))
                return carry

            lax.fori_loop(0, n_z // 2, backward, 0)

    def gradient(t, c):
        def rows_of(i, carry):
            first = pl.multiple_of(i * 256, 256)
            value = jnp.dot(
                counts[t, pl.ds(first, 256), pl.ds(c * span, span)],
                dgot[t, pl.ds(c * span, span), :],
                preferred_element_type=jnp.float32,
            )
            if c > 0:
                value = value + partial[t, pl.ds(first, 256), :]
            partial[t, pl.ds(first, 256), :] = value
            if c == n_chunk - 1:
                part_low[t, pl.ds(first, 256), :] = value.astype(jnp.bfloat16)
            return carry

        lax.fori_loop(0, width // 256, rows_of, 0)

    half = width // CORES
    piece = half // n_y
    kept = pl.ds(pl.multiple_of(core * half, half), half)
    given = pl.ds(pl.multiple_of((1 - core) * half, half), half)
    here = pl.ds(pl.multiple_of(core * half + y * piece, piece), piece)
    last = n_chunk - 1

    for c in range(last):
        bytes_of(direct - 1, 0, tabs, b_recv.at[c]).wait()
        bytes_of(1, 0, tabs, b_own.at[c]).wait()
        for t in range(tabs):
            gradient(t, c)

    for c in range(n_chunk):
        bytes_of(near_both - 1, 0, tabs, e_recv.at[c]).wait()
        bytes_of(1, 0, tabs, e_own.at[c]).wait()
    for t in range(tabs):
        for rows_at in range(0, width, 256):
            total = jnp.zeros((256, dim), jnp.float32)
            for i in range(n_z // 2):
                far = z_pair(i, turn)[1]
                for c in range(n_chunk):
                    block = pl.ds(pl.multiple_of(c * span + far * line, line), line)
                    total = total + jnp.dot(
                        counts_far[t, rows_at : rows_at + 256, block],
                        dfar[t, block, :],
                        preferred_element_type=jnp.float32,
                    )
            far_kept[t, rows_at : rows_at + 256, :] = total
            far_low[t, rows_at : rows_at + 256, :] = total.astype(jnp.bfloat16)
    far_trade = pltpu.make_async_remote_copy(
        src_ref=far_low.at[:, given, :],
        dst_ref=far_half,
        send_sem=i_send,
        recv_sem=i_recv,
        device_id={"rep": sibling},
        device_id_type=MESH,
    )
    far_trade.start()
    far_trade.wait()
    total = far_kept[:, kept, :] + far_half[...].astype(jnp.float32)
    far_half_low[...] = total.astype(jnp.bfloat16)

    def far_scatter(i, carry):
        peer = lax.rem(y + i, n_y)
        pltpu.make_async_remote_copy(
            src_ref=far_half_low.at[:, pl.ds(pl.multiple_of(peer * piece, piece), piece), :],
            dst_ref=far_y.at[y],
            send_sem=j_send,
            recv_sem=j_recv,
            device_id={"rep": peer * CORES + core},
            device_id_type=MESH,
        ).start()
        return carry

    lax.fori_loop(1, n_y, far_scatter, 0)
    far_y[y] = far_half_low[:, pl.ds(pl.multiple_of(y * piece, piece), piece), :]
    far_others = far_y.at[pl.ds(0, n_y - 1)]
    pltpu.make_async_copy(far_others, far_others, j_recv).wait()
    total = far_y[0].astype(jnp.float32)
    for i in range(1, n_y):
        total = total + far_y[i].astype(jnp.float32)
    far_out[...] = total.astype(jnp.bfloat16)
    far_home = pltpu.make_async_remote_copy(
        src_ref=far_out,
        dst_ref=far_in,
        send_sem=k_send,
        recv_sem=k_recv,
        device_id={"shard": opposite},
        device_id_type=MESH,
    )
    far_home.start()

    def trade(t):
        return pltpu.make_async_remote_copy(
            src_ref=part_low.at[t, given, :],
            dst_ref=half_got.at[t],
            send_sem=c_send.at[t],
            recv_sem=c_recv.at[t],
            device_id={"rep": sibling},
            device_id_type=MESH,
        )

    def finish(t):
        return pltpu.make_async_remote_copy(
            src_ref=sums.at[t, kept, :],
            dst_ref=sums.at[t, kept, :],
            send_sem=h_send.at[t],
            recv_sem=h_recv.at[t],
            device_id={"rep": sibling},
            device_id_type=MESH,
        )

    def others(t, sem):
        view = y_got.at[t, pl.ds(0, n_y - 1)]
        return pltpu.make_async_copy(view, view, sem)

    def take(t):
        bytes_of(direct - 1, t, 1, b_recv.at[last + t]).wait()
        bytes_of(1, t, 1, b_own.at[last + t]).wait()
        gradient(t, last)
        trade(t).start()

    def scatter(t):
        trade(t).wait()
        total = partial[t, kept, :] + half_got[t].astype(jnp.float32)
        partial[t, kept, :] = total
        half_low[t] = total.astype(jnp.bfloat16)

        def one_piece(i, carry):
            peer = lax.rem(y + i, n_y)
            pltpu.make_async_remote_copy(
                src_ref=half_low.at[t, pl.ds(pl.multiple_of(peer * piece, piece), piece), :],
                dst_ref=y_got.at[t, y],
                send_sem=y_send.at[t],
                recv_sem=y_recv.at[t],
                device_id={"rep": peer * CORES + core},
                device_id_type=MESH,
            ).start()
            return carry

        lax.fori_loop(1, n_y, one_piece, 0)
        y_got[t, y] = jnp.zeros((piece, dim), jnp.bfloat16)

    def spread(t):
        others(t, y_recv.at[t]).wait()
        total = partial[t, here, :] + far_in[t].astype(jnp.float32)
        for i in range(n_y):
            total = total + y_got[t, i].astype(jnp.float32)
        sums[t, here, :] = total.astype(jnp.bfloat16)

        def one_peer(i, carry):
            peer = lax.rem(y + i, n_y)
            pltpu.make_async_remote_copy(
                src_ref=sums.at[t, here, :],
                dst_ref=sums.at[t, here, :],
                send_sem=g_send.at[t],
                recv_sem=g_recv.at[t],
                device_id={"rep": peer * CORES + core},
                device_id_type=MESH,
            ).start()
            return carry

        lax.fori_loop(1, n_y, one_peer, 0)

    def swap_halves(t):
        others(t, g_recv.at[t]).wait()
        finish(t).start()

    def update(t):
        finish(t).wait()
        summed = sums[t].astype(jnp.float32)
        mean = jnp.sum(summed * summed, axis=1, keepdims=True) * (1.0 / dim)
        scale = learn_rate / (jnp.sqrt(acc_rows[t][:, :1] + mean) + epsilon)
        new[t] = rows[t] - summed * scale
        pltpu.make_async_copy(new.at[t], new_ref.at[t], out_sem.at[n_chunk + t]).start()

    take(0)
    scatter(0)
    far_home.wait()
    spread(0)
    take(1)
    scatter(1)
    swap_halves(0)
    spread(1)
    update(0)
    swap_halves(1)
    update(1)

    lend_rows.wait_send()
    pltpu.make_async_copy(lines, lines, s_send).wait()
    pltpu.make_async_copy(shares, shares, w_send).wait()
    lend_core.wait_send()
    pltpu.make_async_copy(far_others, far_others, j_send).wait()
    for c in range(n_chunk):
        bytes_of(n_shard - 2, 0, tabs, f_send.at[c]).wait()
        bytes_of(near_both - 1, 0, tabs, e_send.at[c]).wait()
        part = pl.ds(c * SUB, SUB)
        pltpu.make_async_copy(inter.at[part], inter_ref.at[0, part], out_sem.at[c]).wait()
    for c in range(last):
        bytes_of(direct - 1, 0, tabs, b_send.at[c]).wait()
    for t in range(tabs):
        bytes_of(direct - 1, t, 1, b_send.at[last + t]).wait()
        others(t, y_send.at[t]).wait()
        others(t, g_send.at[t]).wait()
        pltpu.make_async_copy(new.at[t], new_ref.at[t], out_sem.at[n_chunk + t]).wait()


def local(n_shard, n_rep, emb_table, accumulated, touched, bag_slots, lengths, cotangent):
    tabs, width = touched.shape
    size, dim = emb_table.shape[1:]
    batch = bag_slots.shape[2]
    own = batch // n_shard
    n_tab = tabs * n_shard
    n_chunk = own // SUB
    n_y = n_rep // CORES
    ring = SUB // tabs
    half = width // CORES
    slots = jnp.swapaxes(bag_slots[:, 0], 1, 2)
    dma = pltpu.SemaphoreType.DMA
    low = jnp.bfloat16
    f32 = jnp.float32
    return pl.pallas_call(
        functools.partial(main_kernel, n_shard, n_rep, ring, n_chunk),
        out_shape=(
            jax.ShapeDtypeStruct((1, own, n_tab, n_tab), low),
            jax.ShapeDtypeStruct((tabs, width, dim), f32),
        ),
        in_specs=[HBM, HBM, HBM, VMEM, VMEM, HBM],
        out_specs=(HBM, HBM),
        scratch_shapes=[
            pltpu.VMEM((tabs, size, dim), f32),
            pltpu.SMEM((tabs, size), f32),
            pltpu.SMEM((tabs, width), jnp.int32),
            pltpu.VMEM(slots.shape, jnp.int32),
            pltpu.VMEM((own, n_tab, n_tab), low),
            pltpu.VMEM((own, n_tab, n_tab), low),
            pltpu.VMEM((tabs, width, dim), f32),
            pltpu.VMEM((tabs, width, LANES), f32),
            pltpu.VMEM((tabs, width, dim), low),
            pltpu.VMEM((tabs, width, batch), low),
            pltpu.VMEM((tabs, batch, dim), low),
            pltpu.VMEM((n_tab, own, dim), low),
            pltpu.VMEM((own, n_tab, dim), low),
            pltpu.VMEM((own, n_tab, dim), low),
            pltpu.VMEM((n_tab, own, dim), low),
            pltpu.VMEM((tabs, batch, dim), low),
            pltpu.VMEM((tabs, width, dim), f32),
            pltpu.VMEM((tabs, width, dim), low),
            pltpu.VMEM((tabs, half, dim), low),
            pltpu.VMEM((tabs, half, dim), low),
            pltpu.VMEM((tabs, n_y, half // n_y, dim), low),
            pltpu.VMEM((tabs, width, dim), low),
            pltpu.VMEM((tabs, width, dim), f32),
            pltpu.VMEM((tabs * slots.shape[1], batch), jnp.int16),
            pltpu.VMEM((tabs * slots.shape[1], batch), jnp.int16),
            pltpu.VMEM((tabs, width, dim), low),
            pltpu.VMEM((tabs, width, batch), low),
            pltpu.VMEM((tabs, batch, dim), low),
            pltpu.VMEM((tabs, batch, dim), low),
            pltpu.VMEM((tabs, width, dim), low),
            pltpu.VMEM((tabs, half, dim), low),
            pltpu.VMEM((tabs, width, dim), f32),
            pltpu.VMEM((tabs, half, dim), low),
            pltpu.VMEM((n_y, tabs, half // n_y, dim), low),
            pltpu.VMEM((tabs, half // n_y, dim), low),
            pltpu.VMEM((tabs, half // n_y, dim), low),
            dma((3 + tabs,)),
            dma((n_chunk + tabs,)),
            *[dma((n_chunk,))] * 3,
            *[dma((n_chunk - 1 + tabs,))] * 3,
            *[dma((tabs,))] * 8,
            *[dma((n_chunk,))] * 3,
            *[dma] * 14,
        ],
        compiler_params=pltpu.CompilerParams(
            collective_id=0, has_side_effects=True, vmem_limit_bytes=56 << 20
        ),
    )(emb_table, accumulated, touched, slots, lengths, cotangent)


def solution(mesh):
    return jax.shard_map(
        functools.partial(local, mesh.shape["shard"], mesh.shape["rep"]),
        mesh=mesh,
        in_specs=(
            P("shard", None, None),
            P("shard", None),
            P("shard", None),
            P("shard", "rep", None, None),
            P("shard", "rep", None),
            P("rep", "shard", None, None),
        ),
        out_specs=(P("rep", "shard", None, None), P("shard", None, None)),
        check_vma=False,
    )
```

```python
import functools

import jax
import jax.numpy as jnp
from jax import lax
from jax.experimental import pallas as pl
from jax.experimental.pallas import tpu as pltpu
from jax.sharding import PartitionSpec as P

MESH = pl.DeviceIdType.MESH
VMEM = pl.BlockSpec(memory_space=pltpu.VMEM)
HBM = pl.BlockSpec(memory_space=pl.ANY)
learn_rate = 0.5
epsilon = 1e-08
LANES = 128
SUB = 16
CORES = 2


def main_kernel(
    n_shard, n_rep, ring, n_chunk,
    table_ref, acc_ref, touched_ref, slot_ref, len_ref, cot_ref,
    inter_ref, new_ref,
    table, acc, touched, slots, cot, inter, rows, acc_rows, low, counts, pooled, got, mine, dmine, dsend, dgot,
    partial, part_low, half_got, half_low, y_got, sums, new,
    slots_out, slots_far, low_far, counts_far, pooled_far, dfar,
    far_low, far_half, far_kept, far_half_low, far_y, far_out, far_in,
    in_sem, out_sem, f_send, f_recv, f_own, b_send, b_recv, b_own,
    c_send, c_recv, y_send, y_recv, g_send, g_recv, h_send, h_recv,
    e_send, e_recv, e_own, s_send, s_recv, r_send, r_recv, w_send, w_recv, v_send, v_recv,
    i_send, i_recv, j_send, j_recv, k_send, k_recv,
):
    me = lax.axis_index("shard")
    rep = lax.axis_index("rep")
    core = lax.rem(rep, CORES)
    y = rep // CORES
    z = me // ring
    x = lax.rem(me, ring)
    n_y = n_rep // CORES
    n_z = n_shard // ring
    tabs, width, dim = rows.shape
    batch = slot_ref.shape[2]
    deep = slot_ref.shape[1]
    own = batch // n_shard
    span = batch // n_chunk
    n_tab = tabs * n_shard
    sibling = rep + 1 - 2 * core
    turn = 1 - 2 * core
    opposite = lax.rem(z + n_z // 2, n_z) * ring + lax.rem(x + ring // 2, ring)
    near_x = (0, 1, -1, 2)
    far_x = (4, 5, 3, 6)
    dgot[...] = jnp.zeros_like(dgot)

    loads = [
        pltpu.make_async_copy(touched_ref, touched, in_sem.at[0]),
        pltpu.make_async_copy(acc_ref, acc, in_sem.at[1]),
        *[pltpu.make_async_copy(table_ref.at[t], table.at[t], in_sem.at[2 + t]) for t in range(tabs)],
        pltpu.make_async_copy(cot_ref.at[0], cot, in_sem.at[2 + tabs]),
    ]
    for load in loads:
        load.start()

    barrier = pltpu.get_barrier_semaphore()

    def greet(i, carry):
        pl.semaphore_signal(
            barrier, inc=1, device_id={"shard": lax.rem(me + i, n_shard)}, device_id_type=MESH
        )
        return carry

    lax.fori_loop(1, n_shard, greet, 0)

    def greet_y(i, carry):
        peer = lax.rem(y + i, n_y) * CORES + core
        pl.semaphore_signal(barrier, inc=1, device_id={"rep": peer}, device_id_type=MESH)
        return carry

    lax.fori_loop(1, n_y, greet_y, 0)
    pl.semaphore_signal(barrier, inc=1, device_id={"rep": sibling}, device_id_type=MESH)

    wide = own * ring
    line = wide // n_chunk
    from_lane = lax.broadcasted_iota(jnp.int32, (wide, wide), 0)
    to_lane = lax.broadcasted_iota(jnp.int32, (wide, wide), 1)
    home = lax.rem(to_lane, line) // SUB * own + to_lane // line * SUB + lax.rem(to_lane, SUB)
    sort = jnp.where(from_lane == home, 1.0, 0.0).astype(jnp.bfloat16)

    def sort_slots(r, carry):
        first = pl.multiple_of(r * wide, wide)
        halves = []
        for t in range(tabs):
            ids = slot_ref[t, :, pl.ds(first, wide)]
            sizes = len_ref[t, :, pl.ds(first, wide)]
            place = lax.broadcasted_iota(jnp.int32, ids.shape, 0)
            ids = jnp.where(place < sizes, ids, -1)
            halves += [ids & 255, ids >> 8]
        stack = jnp.concatenate(halves, axis=0).astype(jnp.float32).astype(jnp.bfloat16)
        moved = jnp.dot(stack, sort, preferred_element_type=jnp.float32)
        for t in range(tabs):
            lo = moved[2 * t * deep : (2 * t + 1) * deep]
            hi = moved[(2 * t + 1) * deep : (2 * t + 2) * deep]
            ids = (lo + 256.0 * hi).astype(jnp.int32)
            for c in range(n_chunk):
                lanes = pl.ds(pl.multiple_of(c * span + r * line, line), line)
                slots[t, :, lanes] = ids[:, c * line : (c + 1) * line]
        return carry

    lax.fori_loop(0, n_z, sort_slots, 0)

    key0 = lax.broadcasted_iota(jnp.int32, (SUB, LANES), 0)
    one = jnp.ones((SUB, LANES), jnp.bfloat16)
    zero = jnp.zeros((SUB, LANES), jnp.bfloat16)

    def count(ids, t, to, first):
        each = [
            jnp.broadcast_to(ids[l : l + 1], (SUB, LANES)).astype(jnp.int16) for l in range(deep)
        ]
        for tile in range(width // SUB):
            key = (key0 + tile * SUB).astype(jnp.int16)
            terms = [jnp.where(key == e, one, zero) for e in each]
            while len(terms) > 1:
                terms = [a + b for a, b in zip(terms[::2], terms[1::2])]
            to[t, pl.ds(tile * SUB, SUB), pl.ds(first, LANES)] = terms[0]

    def count_own(t, first):
        count(slots[t, :, pl.ds(first, LANES)], t, counts, first)

    def pool(t, first, made, weights, to):
        to[t, pl.ds(first, LANES), :] = lax.dot_general(
            made[t, :, pl.ds(first, LANES)],
            weights[t],
            (((0,), (0,)), ((), ())),
            preferred_element_type=jnp.float32,
        ).astype(jnp.bfloat16)

    for load in (loads[0], *loads[2 : 2 + tabs]):
        load.wait()
    gathered = width // n_z

    def count_and_gather(r, carry):
        for t in range(tabs):
            for g in range(gathered // SUB):
                base = pl.multiple_of(r * gathered + g * SUB, SUB)
                picked = jnp.concatenate(
                    [
                        table[t, pl.ds(touched[t, r * gathered + g * SUB + u], 1), :]
                        for u in range(SUB)
                    ],
                    axis=0,
                )
                rows[t, pl.ds(base, SUB), :] = picked
                low[t, pl.ds(base, SUB), :] = picked.astype(jnp.bfloat16)
            count_own(t, pl.multiple_of(r * line, line))
        return carry

    lax.fori_loop(0, n_z, count_and_gather, 0)
    pl.semaphore_wait(barrier, n_shard - 1 + n_y - 1 + 1)

    def z_pair(i, way):
        away = lax.rem(i, 2) * ((i + 1) // 2) + (1 - lax.rem(i, 2)) * (n_z - i // 2)
        near = lax.rem(z + way * away + 2 * n_z, n_z)
        return near, lax.rem(near + n_z // 2, n_z)

    def x_at(away, way):
        return lax.rem(x + way * away + 2 * ring, ring)

    share = width // n_y
    lent = pl.ds(pl.multiple_of(y * share, share), share)
    lend_rows = pltpu.make_async_remote_copy(
        src_ref=low.at[core, lent, :],
        dst_ref=low_far.at[core, lent, :],
        send_sem=r_send,
        recv_sem=r_recv,
        device_id={"shard": opposite},
        device_id_type=MESH,
    )
    lend_rows.start()

    pairs = n_z // 4
    far_span = pairs * line
    column = lax.broadcasted_iota(jnp.int32, (deep, line), 1) // SUB
    far_lane = lax.rem(turn * (column - x) + 2 * ring + 5, ring) < ring // 2

    def lend_slots(p, carry):
        for c in range(n_chunk):
            lanes = pl.ds(pl.multiple_of(c * far_span + p * line, line), line)
            for t in range(tabs):
                first, second = (
                    slots[t, :, pl.ds(pl.multiple_of(c * span + r * line, line), line)]
                    for r in (z_pair(2 * p, turn)[1], z_pair(2 * p + 1, turn)[1])
                )
                packed = jnp.where(far_lane, first, pltpu.roll(second, line // 2, 1))
                slots_out[pl.ds(t * deep, deep), lanes] = packed.astype(jnp.int16)
        return carry

    lax.fori_loop(0, pairs, lend_slots, 0)
    lent_slots = pltpu.make_async_remote_copy(
        src_ref=slots_out,
        dst_ref=slots_far,
        send_sem=s_send,
        recv_sem=s_recv,
        device_id={"shard": opposite},
        device_id_type=MESH,
    )
    lent_slots.start()

    def send(src, dst, dest, sent, landed, kept):
        @pl.when(dest == me)
        def _():
            pltpu.make_async_copy(src, dst, kept).start()

        @pl.when(dest != me)
        def _():
            pltpu.make_async_remote_copy(
                src_ref=src,
                dst_ref=dst,
                send_sem=sent,
                recv_sem=landed,
                device_id={"shard": dest},
                device_id_type=MESH,
            ).start()

    def forward(i, carry, c):
        pair = z_pair(i, turn)
        for r in pair:
            for t in range(tabs):
                pool(t, pl.multiple_of(c * span + r * line, line), counts, low, pooled)

        def out(r, column):
            dest = r * ring + column
            send(
                pooled.at[:, pl.ds(c * span + dest * SUB, SUB), :],
                got.at[pl.ds(me * tabs, tabs), pl.ds(c * SUB, SUB), :],
                dest,
                f_send.at[c],
                f_recv.at[c],
                f_own.at[c],
            )

        for j in range(ring // 2):
            out(pair[0], x_at(near_x[j], turn))
            out(pair[1], x_at(-near_x[j], -turn))
            out(pair[0], x_at(far_x[j], turn))
        return carry

    def forward_far(p, carry, c):
        first = pl.multiple_of(c * far_span + p * line, line)
        for t in range(tabs):
            ids = slots_far[pl.ds(t * deep, deep), pl.ds(first, line)].astype(jnp.int32)
            count(ids, t, counts_far, first)
            pool(t, first, counts_far, low_far, pooled_far)
        for j in range(ring // 2):
            dest_x = x_at(near_x[j], turn)
            for odd in range(2):
                place = lax.rem(dest_x + odd * (ring // 2), ring)
                send(
                    pooled_far.at[:, pl.ds(first + place * SUB, SUB), :],
                    got.at[pl.ds(opposite * tabs, tabs), pl.ds(c * SUB, SUB), :],
                    z_pair(2 * p + odd, turn)[0] * ring + dest_x,
                    f_send.at[c],
                    f_recv.at[c],
                    f_own.at[c],
                )
        return carry

    def count_later(r, carry, c):
        for t in range(tabs):
            count_own(t, pl.multiple_of(c * span + r * line, line))
        return carry

    lax.fori_loop(0, n_z // 2, functools.partial(forward, c=0), 0)
    lax.fori_loop(0, n_z // 2, functools.partial(count_later, c=1), 0)
    lend_rows.wait_recv()

    def lend_y(i, carry):
        peer = lax.rem(y + i, n_y)
        pltpu.make_async_remote_copy(
            src_ref=low_far.at[core, lent, :],
            dst_ref=low_far.at[core, lent, :],
            send_sem=w_send,
            recv_sem=w_recv,
            device_id={"rep": peer * CORES + core},
            device_id_type=MESH,
        ).start()
        return carry

    lax.fori_loop(1, n_y, lend_y, 0)
    lax.fori_loop(n_z // 2, n_z, functools.partial(count_later, c=1), 0)
    shares = low_far.at[0, pl.ds(0, (n_y - 1) * share), :]
    pltpu.make_async_copy(shares, shares, w_recv).wait()
    lend_core = pltpu.make_async_remote_copy(
        src_ref=low_far.at[core],
        dst_ref=low_far.at[core],
        send_sem=v_send,
        recv_sem=v_recv,
        device_id={"rep": sibling},
        device_id_type=MESH,
    )
    lend_core.start()
    lax.fori_loop(0, n_z // 4, functools.partial(forward, c=1), 0)
    lent_slots.wait_recv()
    lend_core.wait_recv()
    lax.fori_loop(0, pairs, functools.partial(forward_far, c=0), 0)
    lax.fori_loop(n_z // 4, n_z // 2, functools.partial(forward, c=1), 0)
    lax.fori_loop(0, pairs, functools.partial(forward_far, c=1), 0)

    loads[1].wait()

    def gather_acc(i, carry):
        for t in range(tabs):
            base = pl.multiple_of(i * 8, 8)
            acc_rows[t, pl.ds(base, 8), :] = jnp.concatenate(
                [
                    jnp.full((1, LANES), acc[t, touched[t, i * 8 + u]], jnp.float32)
                    for u in range(8)
                ],
                axis=0,
            )
        return carry

    lax.fori_loop(0, width // 8, gather_acc, 0)
    loads[2 + tabs].wait()

    swap_row = lax.broadcasted_iota(jnp.int32, (SUB * SUB, SUB * SUB), 0)
    swap_col = lax.broadcasted_iota(jnp.int32, (SUB * SUB, SUB * SUB), 1)
    swapped = lax.rem(swap_col, SUB) * SUB + swap_col // SUB
    swap = jnp.where(swap_row == swapped, 1.0, 0.0).astype(jnp.bfloat16)

    def swap_tile(tile):
        flat = tile.reshape(SUB * SUB, dim)
        out = jnp.dot(swap, flat, preferred_element_type=jnp.float32).astype(jnp.bfloat16)
        return out.reshape(SUB, SUB, dim)

    def bytes_of(devices, t0, count_t, sem):
        view = pooled.at[pl.ds(t0, count_t), pl.ds(0, devices * SUB), :]
        return pltpu.make_async_copy(view, view, sem)

    near_both = (n_z // 2) * (ring // 2)
    direct = n_shard - near_both

    def backward(i, carry, c, t):
        pair = z_pair(i, -turn)
        k = t * n_chunk + c

        def out(r, column):
            dest = r * ring + column
            send(
                dsend.at[pl.ds(dest * tabs + t, 1), pl.ds(c * SUB, SUB), :],
                dgot.at[pl.ds(t, 1), pl.ds(c * span + me * SUB, SUB), :],
                dest,
                b_send.at[k],
                b_recv.at[k],
                b_own.at[k],
            )

        for u in range(ring // 2):
            out(pair[0], x_at(near_x[u], -turn))
            out(pair[1], x_at(-near_x[u], turn))
            out(pair[0], x_at(far_x[u], -turn))
        return carry

    for c in range(n_chunk):
        bytes_of(n_shard - 2, 0, tabs, f_recv.at[c]).wait()
        bytes_of(2, 0, tabs, f_own.at[c]).wait()
        part = pl.ds(c * SUB, SUB)

        def to_samples(g, carry, part=part):
            first = pl.multiple_of(g * SUB, SUB)
            mine[part, pl.ds(first, SUB), :] = swap_tile(got[pl.ds(first, SUB), part, :])
            return carry

        lax.fori_loop(0, n_tab // SUB, to_samples, 0, unroll=2)

        def sample(i, carry, c=c):
            for u in range(4):
                b = c * SUB + i * 4 + u
                vectors = mine[b]
                inter[b] = lax.dot_general(
                    vectors, vectors, (((1,), (1,)), ((), ())), preferred_element_type=jnp.float32
                ).astype(jnp.bfloat16)
                both = jnp.concatenate([cot[b], cot[b].T], axis=1)
                dmine[b] = jnp.dot(
                    both,
                    jnp.concatenate([vectors, vectors], axis=0),
                    preferred_element_type=jnp.float32,
                ).astype(jnp.bfloat16)
            return carry

        lax.fori_loop(0, SUB // 4, sample, 0)
        pltpu.make_async_copy(inter.at[part], inter_ref.at[0, part], out_sem.at[c]).start()

        def to_tables(g, carry, part=part):
            first = pl.multiple_of(g * SUB, SUB)
            dsend[pl.ds(first, SUB), part, :] = swap_tile(dmine[part, pl.ds(first, SUB), :])
            return carry

        lax.fori_loop(0, n_tab // SUB, to_tables, 0, unroll=2)

        def backward_far(i, carry, c=c):
            near, far = z_pair(i, -turn)
            place = lax.rem(x + lax.rem(i, 2) * (ring // 2), ring)
            for j in range(ring // 2):
                home_x = x_at(far_x[j], -turn)
                send(
                    dsend.at[pl.ds((far * ring + home_x) * tabs, tabs), pl.ds(c * SUB, SUB), :],
                    dfar.at[:, pl.ds(c * far_span + i // 2 * line + place * SUB, SUB), :],
                    near * ring + lax.rem(home_x + ring // 2, ring),
                    e_send.at[c],
                    e_recv.at[c],
                    e_own.at[c],
                )
            return carry

        lax.fori_loop(0, n_z // 2, backward_far, 0)

        for t in range(tabs):
            for sent in [c] if t == 0 else range(n_chunk) if c == n_chunk - 1 else []:
                lax.fori_loop(0, n_z // 2, functools.partial(backward, c=sent, t=t), 0)

    def gradient(t, c):
        def rows_of(i, carry):
            first = pl.multiple_of(i * 256, 256)
            value = jnp.dot(
                counts[t, pl.ds(first, 256), pl.ds(c * span, span)],
                dgot[t, pl.ds(c * span, span), :],
                preferred_element_type=jnp.float32,
            )
            if c > 0:
                value = value + partial[t, pl.ds(first, 256), :]
            partial[t, pl.ds(first, 256), :] = value
            if c == n_chunk - 1:
                part_low[t, pl.ds(first, 256), :] = value.astype(jnp.bfloat16)
            return carry

        lax.fori_loop(0, width // 256, rows_of, 0)

    half = width // CORES
    piece = half // n_y
    kept = pl.ds(pl.multiple_of(core * half, half), half)
    given = pl.ds(pl.multiple_of((1 - core) * half, half), half)
    here = pl.ds(pl.multiple_of(core * half + y * piece, piece), piece)
    last = n_chunk - 1

    def take(t, c):
        bytes_of(direct - 1, t, 1, b_recv.at[t * n_chunk + c]).wait()
        bytes_of(1, t, 1, b_own.at[t * n_chunk + c]).wait()
        gradient(t, c)

    for c in range(last):
        take(0, c)

    for c in range(n_chunk):
        bytes_of(near_both - 1, 0, tabs, e_recv.at[c]).wait()
        bytes_of(1, 0, tabs, e_own.at[c]).wait()
    for t in range(tabs):
        for rows_at in range(0, width, 256):
            total = jnp.dot(
                counts_far[t, rows_at : rows_at + 256, :], dfar[t], preferred_element_type=jnp.float32
            )
            far_kept[t, rows_at : rows_at + 256, :] = total
            far_low[t, rows_at : rows_at + 256, :] = total.astype(jnp.bfloat16)
    far_trade = pltpu.make_async_remote_copy(
        src_ref=far_low.at[:, given, :],
        dst_ref=far_half,
        send_sem=i_send,
        recv_sem=i_recv,
        device_id={"rep": sibling},
        device_id_type=MESH,
    )
    far_trade.start()
    far_trade.wait()
    total = far_kept[:, kept, :] + far_half[...].astype(jnp.float32)
    far_half_low[...] = total.astype(jnp.bfloat16)

    def far_scatter(i, carry):
        peer = lax.rem(y + i, n_y)
        pltpu.make_async_remote_copy(
            src_ref=far_half_low.at[:, pl.ds(pl.multiple_of(peer * piece, piece), piece), :],
            dst_ref=far_y.at[y],
            send_sem=j_send,
            recv_sem=j_recv,
            device_id={"rep": peer * CORES + core},
            device_id_type=MESH,
        ).start()
        return carry

    lax.fori_loop(1, n_y, far_scatter, 0)
    far_y[y] = far_half_low[:, pl.ds(pl.multiple_of(y * piece, piece), piece), :]
    far_others = far_y.at[pl.ds(0, n_y - 1)]
    far_home = pltpu.make_async_remote_copy(
        src_ref=far_out,
        dst_ref=far_in,
        send_sem=k_send,
        recv_sem=k_recv,
        device_id={"shard": opposite},
        device_id_type=MESH,
    )

    def send_home():
        pltpu.make_async_copy(far_others, far_others, j_recv).wait()
        total = far_y[0].astype(jnp.float32)
        for i in range(1, n_y):
            total = total + far_y[i].astype(jnp.float32)
        far_out[...] = total.astype(jnp.bfloat16)
        far_home.start()

    def trade(t):
        return pltpu.make_async_remote_copy(
            src_ref=part_low.at[t, given, :],
            dst_ref=half_got.at[t],
            send_sem=c_send.at[t],
            recv_sem=c_recv.at[t],
            device_id={"rep": sibling},
            device_id_type=MESH,
        )

    def finish(t):
        return pltpu.make_async_remote_copy(
            src_ref=sums.at[t, kept, :],
            dst_ref=sums.at[t, kept, :],
            send_sem=h_send.at[t],
            recv_sem=h_recv.at[t],
            device_id={"rep": sibling},
            device_id_type=MESH,
        )

    def others(t, sem):
        view = y_got.at[t, pl.ds(0, n_y - 1)]
        return pltpu.make_async_copy(view, view, sem)

    def scatter(t):
        trade(t).wait()
        total = partial[t, kept, :] + half_got[t].astype(jnp.float32)
        partial[t, kept, :] = total
        half_low[t] = total.astype(jnp.bfloat16)

        def one_piece(i, carry):
            peer = lax.rem(y + i, n_y)
            pltpu.make_async_remote_copy(
                src_ref=half_low.at[t, pl.ds(pl.multiple_of(peer * piece, piece), piece), :],
                dst_ref=y_got.at[t, y],
                send_sem=y_send.at[t],
                recv_sem=y_recv.at[t],
                device_id={"rep": peer * CORES + core},
                device_id_type=MESH,
            ).start()
            return carry

        lax.fori_loop(1, n_y, one_piece, 0)
        y_got[t, y] = jnp.zeros((piece, dim), jnp.bfloat16)

    def spread(t):
        others(t, y_recv.at[t]).wait()
        total = partial[t, here, :] + far_in[t].astype(jnp.float32)
        for i in range(n_y):
            total = total + y_got[t, i].astype(jnp.float32)
        sums[t, here, :] = total.astype(jnp.bfloat16)

        def one_peer(i, carry):
            peer = lax.rem(y + i, n_y)
            pltpu.make_async_remote_copy(
                src_ref=sums.at[t, here, :],
                dst_ref=sums.at[t, here, :],
                send_sem=g_send.at[t],
                recv_sem=g_recv.at[t],
                device_id={"rep": peer * CORES + core},
                device_id_type=MESH,
            ).start()
            return carry

        lax.fori_loop(1, n_y, one_peer, 0)

    def swap_halves(t):
        others(t, g_recv.at[t]).wait()
        finish(t).start()

    def update(t):
        finish(t).wait()
        summed = sums[t].astype(jnp.float32)
        mean = jnp.sum(summed * summed, axis=1, keepdims=True) * (1.0 / dim)
        scale = learn_rate / (jnp.sqrt(acc_rows[t][:, :1] + mean) + epsilon)
        new[t] = rows[t] - summed * scale
        pltpu.make_async_copy(new.at[t], new_ref.at[t], out_sem.at[n_chunk + t]).start()

    take(0, last)
    trade(0).start()
    send_home()
    scatter(0)
    for c in range(last):
        take(1, c)
    far_home.wait()
    spread(0)
    take(1, last)
    trade(1).start()
    scatter(1)
    swap_halves(0)
    spread(1)
    update(0)
    swap_halves(1)
    update(1)

    lend_rows.wait_send()
    lent_slots.wait_send()
    pltpu.make_async_copy(shares, shares, w_send).wait()
    lend_core.wait_send()
    pltpu.make_async_copy(far_others, far_others, j_send).wait()
    for c in range(n_chunk):
        bytes_of(n_shard - 2, 0, tabs, f_send.at[c]).wait()
        bytes_of(near_both - 1, 0, tabs, e_send.at[c]).wait()
        part = pl.ds(c * SUB, SUB)
        pltpu.make_async_copy(inter.at[part], inter_ref.at[0, part], out_sem.at[c]).wait()
    for t in range(tabs):
        for c in range(n_chunk):
            bytes_of(direct - 1, t, 1, b_send.at[t * n_chunk + c]).wait()
        others(t, y_send.at[t]).wait()
        others(t, g_send.at[t]).wait()
        pltpu.make_async_copy(new.at[t], new_ref.at[t], out_sem.at[n_chunk + t]).wait()


def hand_over(interaction, new_rows):
    def kernel(inter, new, inter_out, new_out):
        inter_out[...] = inter[...]
        new_out[...] = new[...]

    _, own, n_tab, _ = interaction.shape
    tabs, width, dim = new_rows.shape
    steps = 4
    specs = (
        pl.BlockSpec((1, own // steps, n_tab, n_tab), lambda i: (0, i, 0, 0)),
        pl.BlockSpec((tabs, width // steps, dim), lambda i: (0, i, 0)),
    )
    return pl.pallas_call(
        kernel,
        grid=(steps,),
        out_shape=tuple(jax.ShapeDtypeStruct(a.shape, a.dtype) for a in (interaction, new_rows)),
        in_specs=specs,
        out_specs=specs,
        compiler_params=pltpu.CompilerParams(vmem_limit_bytes=60 << 20),
    )(interaction, new_rows)


def local(n_shard, n_rep, emb_table, accumulated, touched, bag_slots, lengths, cotangent):
    tabs, width = touched.shape
    size, dim = emb_table.shape[1:]
    batch = bag_slots.shape[2]
    own = batch // n_shard
    n_tab = tabs * n_shard
    n_chunk = own // SUB
    n_y = n_rep // CORES
    ring = SUB // tabs
    half = width // CORES
    slots = jnp.swapaxes(bag_slots[:, 0], 1, 2)
    dma = pltpu.SemaphoreType.DMA
    low = jnp.bfloat16
    f32 = jnp.float32
    results = pl.pallas_call(
        functools.partial(main_kernel, n_shard, n_rep, ring, n_chunk),
        out_shape=(
            jax.ShapeDtypeStruct((1, own, n_tab, n_tab), low),
            jax.ShapeDtypeStruct((tabs, width, dim), f32),
        ),
        in_specs=[HBM, HBM, HBM, VMEM, VMEM, HBM],
        out_specs=(HBM, HBM),
        scratch_shapes=[
            pltpu.VMEM((tabs, size, dim), f32),
            pltpu.SMEM((tabs, size), f32),
            pltpu.SMEM((tabs, width), jnp.int32),
            pltpu.VMEM(slots.shape, jnp.int32),
            pltpu.VMEM((own, n_tab, n_tab), low),
            pltpu.VMEM((own, n_tab, n_tab), low),
            pltpu.VMEM((tabs, width, dim), f32),
            pltpu.VMEM((tabs, width, LANES), f32),
            pltpu.VMEM((tabs, width, dim), low),
            pltpu.VMEM((tabs, width, batch), low),
            pltpu.VMEM((tabs, batch, dim), low),
            pltpu.VMEM((n_tab, own, dim), low),
            pltpu.VMEM((own, n_tab, dim), low),
            pltpu.VMEM((own, n_tab, dim), low),
            pltpu.VMEM((n_tab, own, dim), low),
            pltpu.VMEM((tabs, batch, dim), low),
            pltpu.VMEM((tabs, width, dim), f32),
            pltpu.VMEM((tabs, width, dim), low),
            pltpu.VMEM((tabs, half, dim), low),
            pltpu.VMEM((tabs, half, dim), low),
            pltpu.VMEM((tabs, n_y, half // n_y, dim), low),
            pltpu.VMEM((tabs, width, dim), low),
            pltpu.VMEM((tabs, width, dim), f32),
            pltpu.VMEM((tabs * slots.shape[1], batch // 4), jnp.int16),
            pltpu.VMEM((tabs * slots.shape[1], batch // 4), jnp.int16),
            pltpu.VMEM((tabs, width, dim), low),
            pltpu.VMEM((tabs, width, batch // 4), low),
            pltpu.VMEM((tabs, batch // 4, dim), low),
            pltpu.VMEM((tabs, batch // 4, dim), low),
            pltpu.VMEM((tabs, width, dim), low),
            pltpu.VMEM((tabs, half, dim), low),
            pltpu.VMEM((tabs, width, dim), f32),
            pltpu.VMEM((tabs, half, dim), low),
            pltpu.VMEM((n_y, tabs, half // n_y, dim), low),
            pltpu.VMEM((tabs, half // n_y, dim), low),
            pltpu.VMEM((tabs, half // n_y, dim), low),
            dma((3 + tabs,)),
            dma((n_chunk + tabs,)),
            *[dma((n_chunk,))] * 3,
            *[dma((n_chunk * tabs,))] * 3,
            *[dma((tabs,))] * 8,
            *[dma((n_chunk,))] * 3,
            *[dma] * 14,
        ],
        compiler_params=pltpu.CompilerParams(
            collective_id=0, has_side_effects=True, vmem_limit_bytes=56 << 20
        ),
    )(emb_table, accumulated, touched, slots, lengths, cotangent)
    return hand_over(*results)


def solution(mesh):
    return jax.shard_map(
        functools.partial(local, mesh.shape["shard"], mesh.shape["rep"]),
        mesh=mesh,
        in_specs=(
            P("shard", None, None),
            P("shard", None),
            P("shard", None),
            P("shard", "rep", None, None),
            P("shard", "rep", None),
            P("rep", "shard", None, None),
        ),
        out_specs=(P("rep", "shard", None, None), P("shard", None, None)),
        check_vma=False,
    )
```
